32 devices in a mesh: groups: 2 (over x), users: 16 (over z, y, core).
Axes of the slice: x: 2, y: 2, z: 4, core: 2. Of those that a mesh axis runs over, the one named last changes fastest.
Arguments:
- history: bfloat16 [32, 512, 1024], P(('groups', 'users')), parts along dimension 0, may hold values from -6 to 6
- hist_len: int32 [32], P(('groups', 'users')), parts along dimension 0, may hold values from 128 to 512, as said below
- candidates: bfloat16 [8192, 1024], P(('groups', 'users')), parts along dimension 0, may hold values from -6 to 6
- cand_user: int32 [8192, 1], P(('groups', 'users')), parts along dimension 0, may hold values from 0 to 15; in each aligned block of 256 rows (0 to 255, 256 to 511, ...) at most 32 rows name the same one
- cand_task: int32 [8192], P(('groups', 'users')), parts along dimension 0, may hold values from 0 to 2
- kv_weight: bfloat16 [1024, 2048], replicated, may hold values from -1 to 1
- query_weight: bfloat16 [1024, 1024], replicated, may hold values from -1 to 1
- out_weight: bfloat16 [1024, 1024], replicated, may hold values from -0.75 to 0.75
- head_weight: bfloat16 [1024, 3], replicated, may hold values from -0.1875 to 0.1875
Outputs:
- new_history: bfloat16 [32, 512, 1024], P(('groups', 'users')), parts along dimension 0
- scores: float32 [8192], P(('groups', 'users')), parts along dimension 0
The draws below stay inside these ranges and needn't reach their ends.
There are 2 independent parts, one for each index of `groups`. The reference program is written for one: setup_inputs(seed, part) draws one part's arguments, and reference() takes and returns one part's arrays. A program takes and returns all parts, laid end to end along the dimension named above; an argument that names none is the same for every part. Nothing has to cross between parts.
Inputs may be any that keep to these rules, and one draw needn't show every extreme that they name: `hist_len`: each history holds a whole number of pages of 128 events, and some user has all 512. `cand_user`: among the slots of one device no user is named more than 32 times; on some device some user is named exactly 32 times.
All inputs are finite; a program needn't handle non-finite values.
Results may differ from the reference program's by a relative error of at most 0.012.
The reference program's roundings to bfloat16 on the way count: a program that leaves them out, or rounds other values in their place, can miss the bound.
Values may be sent and summed in bfloat16 or wider, within the bound.
A program may use at most 192 MiB of HBM per device.

```python
import math
import jax
import jax.numpy as jnp
import numpy as np
from jax import lax

D = 1024
HEADS = 16
HEAD_DIM = 64
TASKS = 3
PAGE = 128
HIST = 512
SLOT_DEV = 256
USERS = 16
SLOTS = 4096
MOST = 32


def draw_hist_len(key, part):
    key = jax.random.fold_in(key, 11)
    page_count = jax.random.randint(jax.random.fold_in(key, 1), (USERS,), 1, HIST // PAGE + 1)
    longest = jax.random.randint(jax.random.fold_in(key, 2), (), 0, USERS)
    page_count = jnp.where(jnp.arange(USERS) == longest, HIST // PAGE, page_count)
    return (page_count * PAGE).astype(jnp.int32)


def draw_history(key, part):
    key = jax.random.fold_in(key, 17)
    base = jnp.clip(jax.random.normal(jax.random.fold_in(key, 1), (USERS, HIST, D), jnp.float32), -6.0, 6.0)
    return base.astype(jnp.bfloat16)


def draw_candidates(key, part):
    key = jax.random.fold_in(key, 23)
    base = jnp.clip(jax.random.normal(jax.random.fold_in(key, 1), (SLOTS, D), jnp.float32), -6.0, 6.0)
    return base.astype(jnp.bfloat16)


def draw_query_weight(key, part):
    own_key = jax.random.fold_in(key, 29)
    matrix = jnp.clip(jax.random.normal(own_key, (D, D), jnp.float32), -6.0, 6.0) * D ** (-0.5)
    return matrix.astype(jnp.bfloat16)


def draw_kv_weight(key, part):
    own_key = jax.random.fold_in(key, 31)
    matrix = jnp.clip(jax.random.normal(own_key, (D, 2 * D), jnp.float32), -6.0, 6.0) * D ** (-0.5)
    return matrix.astype(jnp.bfloat16)


def touch_ends(result, stream_key, least, largest):
    extent = result.shape
    spot = [jax.random.randint(jax.random.fold_in(stream_key, axis), (), 0, extent[axis]) for axis in range(len(extent))]
    result = result.at[tuple(spot)].set(least)
    longest = extent.index(max(extent))
    spot[longest] = (spot[longest] + 1) % extent[longest]
    return result.at[tuple(spot)].set(largest)


def deal_out(rng, own, number, rows, amount, top, limit, lean):
    ranking = jax.random.permutation(rng, amount)
    crowded, ordinary = shares(amount, rows * top, limit, lean, True), shares(amount, rows * top, limit, lean, False)
    places = jnp.arange(amount)

    def named(lengths, offset_by):
        used = int((lengths > 0).sum())
        fixed = max(1, used // 4)
        passed = fixed + (places - fixed + offset_by * (used - fixed)) % max(1, amount - fixed)
        return jnp.zeros((amount,), jnp.int32).at[ranking[jnp.where(places < fixed, places, passed)]].set(jnp.asarray(lengths, jnp.int32))

    lengths = jnp.where(number % 4 == 0, named(crowded, number // 4), named(ordinary, number - number // 4 - 1))
    mixed = jax.random.permutation(jax.random.fold_in(own, 3), amount)
    source_of, receiver = mixed[0:amount // 2 * 2:2], mixed[1:amount // 2 * 2:2]
    slack = jnp.minimum(lengths[source_of] - 1, limit - lengths[receiver]) // 2
    slack = jnp.where((source_of == ranking[0]) | (receiver == ranking[0]) | (lengths[receiver] == 0), 0, jnp.maximum(slack, 0))
    passed = jax.random.randint(jax.random.fold_in(own, 4), (amount // 2,), 0, 1 << 20) % (slack + 1)
    lengths = lengths.at[source_of].add(-passed).at[receiver].add(passed)
    items = jnp.searchsorted(jnp.cumsum(lengths), jnp.arange(rows * top), side="right").astype(jnp.int32)
    listing = items.reshape(top, rows).T
    listing = listing[jax.random.permutation(jax.random.fold_in(own, 1), rows)]
    offset_by = jax.random.randint(jax.random.fold_in(own, 2), (rows, 1), 0, top)
    return jnp.take_along_axis(listing, (jnp.arange(top)[None, :] + offset_by) % top, axis=1)


def shares(number_of, total, reach, slope, full):
    loads = [(1 << 20) // math.isqrt(standing ** slope) + 1 for standing in range(1, number_of + 1)]
    largest = reach if full else min(reach, max(-(-total // number_of), total * loads[0] // sum(loads)))
    least = 1 if total - largest >= number_of - 1 else 0
    given, surplus = [largest] + [least] * (number_of - 1), total - largest - least * (number_of - 1)
    while surplus > 0:
        free = [i for i in range(1, number_of) if given[i] < largest] or [i for i in range(1, number_of) if given[i] < reach]
        mass, left = sum([loads[i] for i in free]), surplus
        for i in free:
            addition = min(reach - given[i], max(1, left * loads[i] // mass), surplus)
            given[i] = given[i] + addition
            surplus = surplus - addition
    return np.array(given)


def centred(rng, dims, scale, most, held_as=jnp.bfloat16):
    return jnp.clip(scale * jax.random.normal(rng, dims, jnp.float32), -most, most).astype(held_as)


def setup_inputs(seed: int = 0, part: int = 0) -> dict:
    keys = jax.random.split(jax.random.key(seed), 10)
    part_splits = jax.random.split(jax.random.fold_in(keys[9], part), 10)
    history = draw_history(jax.random.fold_in(jax.random.fold_in(keys[9], part), 71), part)
    hist_len = draw_hist_len(jax.random.fold_in(jax.random.fold_in(keys[9], part), 71), part)
    candidates = draw_candidates(jax.random.fold_in(jax.random.fold_in(keys[9], part), 71), part)
    cand_user_keys = jax.random.split(jax.random.fold_in(part_splits[3], 1), SLOTS // SLOT_DEV)
    cand_user_turns = jax.random.permutation(jax.random.fold_in(part_splits[3], 3), SLOTS // SLOT_DEV)
    cand_user = jax.vmap(lambda own, number: deal_out(jax.random.fold_in(part_splits[3], 2), own, number, SLOT_DEV, USERS, 1, MOST, 2))(cand_user_keys, cand_user_turns).reshape((SLOTS, 1))
    cand_task = touch_ends(jax.random.randint(part_splits[4], (SLOTS,), 0, TASKS), jax.random.fold_in(part_splits[4], 1), 0, TASKS - 1).astype(jnp.int32)
    kv_weight = draw_kv_weight(jax.random.fold_in(keys[9], 71), part)
    query_weight = draw_query_weight(jax.random.fold_in(keys[9], 71), part)
    out_weight = centred(keys[7], (D, D), (D // 16) ** -0.5, 0.75)
    head_weight = centred(keys[8], (D, TASKS), D ** -0.5, 0.1875)
    return {"history": history, "hist_len": hist_len, "candidates": candidates, "cand_user": cand_user, "cand_task": cand_task, "kv_weight": kv_weight, "query_weight": query_weight, "out_weight": out_weight, "head_weight": head_weight}


epsilon = 1e-06

def normalize(values):
    values = values.astype(jnp.float32)
    return values * lax.rsqrt(lax.optimization_barrier(jnp.mean(values * values, axis=-1, keepdims=True)) + epsilon)

def attend(queries, key_rows, value_rows, allowed):
    queries, key_rows, value_rows = lax.optimization_barrier((queries, key_rows, value_rows))
    query_count = queries.shape[0]
    events = key_rows.shape[0]
    query_heads = queries.astype(jnp.float32).reshape(query_count, HEADS, HEAD_DIM)
    key_heads = key_rows.astype(jnp.float32).reshape(events, HEADS, HEAD_DIM)
    value_heads = value_rows.astype(jnp.float32).reshape(events, HEADS, HEAD_DIM)
    scores = jnp.einsum('rhd,khd->hrk', query_heads, key_heads) * HEAD_DIM ** (-0.5)
    scores = jnp.where(allowed[None, :, :], scores, -jnp.inf)
    highest = lax.optimization_barrier(jnp.max(scores, axis=-1, keepdims=True))
    raised = jnp.exp(scores - highest)
    weights = (raised / lax.optimization_barrier(jnp.sum(raised, axis=-1, keepdims=True))).astype(jnp.bfloat16)
    weights = lax.optimization_barrier(weights)
    context = jnp.einsum('hrk,khd->rhd', weights.astype(jnp.float32), value_heads)
    return context.reshape(query_count, HEADS * HEAD_DIM).astype(jnp.bfloat16)

def reference(history, hist_len, candidates, cand_user, cand_task, kv_weight, query_weight, out_weight, head_weight):
    position = jnp.arange(HIST)

    def encode(inputs):
        user_events, length = inputs
        normed = normalize(user_events).astype(jnp.bfloat16)
        joined_kv = jnp.dot(normed, kv_weight, preferred_element_type=jnp.float32).astype(jnp.bfloat16)
        key_rows = joined_kv[:, :D]
        value_rows = joined_kv[:, D:]
        queries = jnp.dot(normed, query_weight, preferred_element_type=jnp.float32).astype(jnp.bfloat16)
        allowed = (position[None, :] <= position[:, None]) & (position[None, :] < length)
        context = attend(queries, key_rows, value_rows, allowed)
        updated = user_events.astype(jnp.float32) + jnp.dot(context, out_weight, preferred_element_type=jnp.float32)
        return (updated.astype(jnp.bfloat16), key_rows, value_rows)
    new_history, all_keys, all_values = lax.map(encode, (history, hist_len))
    cand_queries = jnp.dot(normalize(candidates).astype(jnp.bfloat16), query_weight, preferred_element_type=jnp.float32).astype(jnp.bfloat16)
    owners = cand_user[:, 0].astype(jnp.int32)
    sort_order = jnp.argsort(owners, stable=True).astype(jnp.int32)
    counts = lax.optimization_barrier(jnp.sum((owners[:, None] == jnp.arange(USERS)[None, :]).astype(jnp.int32), axis=0)).astype(jnp.int32)
    starts = (jnp.cumsum(counts) - counts).astype(jnp.int32)
    capacity = USERS * MOST
    sorted_queries = jnp.concatenate([cand_queries[sort_order], jnp.zeros((capacity, D), jnp.bfloat16)], axis=0)

    def visit_user(buffer, inputs):
        first_row, live_rows, length, key_rows, value_rows = inputs
        user_block = lax.dynamic_slice_in_dim(sorted_queries, first_row, capacity, 0)
        allowed = jnp.broadcast_to(position[None, :] < length, (capacity, HIST))
        context = attend(user_block, key_rows, value_rows, allowed)
        live_mask = jnp.arange(capacity)[:, None] < live_rows
        context = jnp.where(live_mask, context, jnp.zeros_like(context))
        return (lax.dynamic_update_slice_in_dim(buffer, context, first_row, 0), None)
    buffer, unused = lax.scan(visit_user, jnp.zeros((SLOTS + capacity, D), jnp.bfloat16), (starts, counts, hist_len, all_keys, all_values))
    gathered = jnp.zeros((SLOTS, D), jnp.bfloat16).at[sort_order].set(buffer[:SLOTS])
    combined = candidates.astype(jnp.float32) + jnp.dot(gathered, out_weight, preferred_element_type=jnp.float32)
    logits = jnp.dot(normalize(combined).astype(jnp.bfloat16), head_weight, preferred_element_type=jnp.float32)
    chosen = cand_task[:, None] == jnp.arange(TASKS)[None, :]
    scores = lax.optimization_barrier(jnp.sum(jnp.where(chosen, logits, jnp.zeros_like(logits)), axis=1))
    return (new_history, scores)
```

```python
import functools

import jax
import jax.numpy as jnp
from jax import lax
from jax.experimental import pallas as pl
from jax.experimental.pallas import tpu as pltpu
from jax.sharding import PartitionSpec as P

HEADS = 16
LANES = 128
EPSILON = 1e-06
NEG = -1e30
F32 = jnp.float32
BF16 = jnp.bfloat16
MESH = pl.DeviceIdType.MESH


def normed_rows(values):
    values = values.astype(F32)
    mean = jnp.mean(values * values, axis=-1, keepdims=True)
    return (values * lax.rsqrt(mean + EPSILON)).astype(BF16)


def dot_t(a, b):
    return lax.dot_general(a, b, (((1,), (1,)), ((), ())), preferred_element_type=F32)


def dot(a, b):
    return jnp.dot(a, b, preferred_element_type=F32)


def kernel(
    peers,
    cap,
    chunk,
    len_ref,
    user_ref,
    task_ref,
    cand_ref,
    head_ref,
    hist_hbm,
    kvw_hbm,
    qw_hbm,
    ow_hbm,
    new_hbm,
    score_ref,
    hist,
    kvw,
    qw,
    ow,
    new,
    normed,
    keys,
    values,
    queries,
    context,
    bias,
    outbox,
    inbox,
    cand_queries,
    cand_context,
    logit_out,
    logit_in,
    load_sem,
    send_sem,
    recv_sem,
    back_send_sem,
    back_recv_sem,
):
    me = lax.axis_index("users")
    half_peers = peers // 2
    events, features = hist.shape
    slots = inbox.shape[0]
    rows = cand_ref.shape[0]
    pairs = features // LANES
    half = me // half_peers

    loads = [
        pltpu.make_async_copy(src, dst, load_sem.at[i])
        for i, (src, dst) in enumerate(
            ((hist_hbm.at[0], hist), (kvw_hbm, kvw), (qw_hbm, qw), (ow_hbm, ow))
        )
    ]
    for load in loads:
        load.start()

    barrier = pltpu.get_barrier_semaphore()

    def greet(i, carry):
        pl.semaphore_signal(
            barrier, inc=1, device_id={"users": lax.rem(me + i, peers)}, device_id_type=MESH
        )
        return carry

    lax.fori_loop(1, peers, greet, 0)

    row_id = lax.broadcasted_iota(jnp.int32, (rows, rows), 0)
    col_id = lax.broadcasted_iota(jnp.int32, (rows, rows), 1)
    eye = row_id == col_id
    user_row = user_ref[...].astype(F32)
    task_row = task_ref[...].astype(F32)
    user_col = jnp.sum(jnp.where(eye, user_row, 0.0), axis=1, keepdims=True)
    task_col = jnp.sum(jnp.where(eye, task_row, 0.0), axis=1, keepdims=True)
    same = user_col == user_row
    rank_row = jnp.sum(jnp.where(same & (row_id < col_id), 1.0, 0.0), axis=0, keepdims=True)
    rank_col = jnp.sum(jnp.where(same & (col_id < row_id), 1.0, 0.0), axis=1, keepdims=True)
    target_row = user_row * cap + rank_row

    def pack(first):
        slot = (lax.broadcasted_iota(jnp.int32, (chunk, rows), 0) + first).astype(F32)
        chosen = jnp.where(slot == target_row, 1.0, 0.0).astype(BF16)
        outbox[pl.ds(first, chunk), :] = dot(chosen, cand_ref[...]).astype(BF16)

    def block(ref, peer):
        return ref.at[pl.ds(pl.multiple_of(peer * cap, cap), cap), :]

    def sending(peer):
        return pltpu.make_async_remote_copy(
            src_ref=block(outbox, peer),
            dst_ref=block(inbox, me),
            send_sem=send_sem.at[peer],
            recv_sem=recv_sem.at[me],
            device_id={"users": peer},
            device_id_type=MESH,
        )

    def receiving(peer):
        return pltpu.make_async_remote_copy(
            src_ref=block(outbox, peer),
            dst_ref=block(inbox, peer),
            send_sem=send_sem.at[peer],
            recv_sem=recv_sem.at[peer],
            device_id={"users": peer},
            device_id_type=MESH,
        )

    half_chunks = slots // 2 // chunk
    far = 1 - half

    def pack_half(which):
        def step(i, carry):
            pack(pl.multiple_of(which * (slots // 2) + i * chunk, chunk))
            return carry

        lax.fori_loop(0, half_chunks, step, 0)

    pack_half(far)
    pl.semaphore_wait(barrier, peers - 1)

    def send_far(i, carry):
        sending(far * half_peers + lax.rem(me + i, half_peers)).start()
        return carry

    lax.fori_loop(0, half_peers, send_far, 0)
    pack_half(half)

    def send_near(i, carry):
        sending(half * half_peers + lax.rem(me + i, half_peers)).start()
        return carry

    lax.fori_loop(1, half_peers, send_near, 0)
    own = pl.ds(pl.multiple_of(me * cap, cap), cap)
    inbox[own, :] = outbox[own, :]

    loads[0].wait()
    normed[...] = normed_rows(hist[...])
    event_row = lax.broadcasted_iota(jnp.int32, (events, events), 0)
    event_col = lax.broadcasted_iota(jnp.int32, (events, events), 1)
    allowed = (event_col <= event_row) & (event_col < len_ref[0])
    bias[...] = jnp.where(allowed, 0.0, NEG)
    scale = 0.125
    low = lax.broadcasted_iota(jnp.int32, (events, LANES), 1) < LANES // 2
    loads[1].wait()
    loads[2].wait()

    def project(i, carry):
        cols = pl.ds(pl.multiple_of(i * 256, 256), 256)
        later = pl.ds(pl.multiple_of(features + i * 256, 256), 256)
        n = normed[...]
        k = dot(n, kvw[:, cols])
        v = dot(n, kvw[:, later])
        q = dot(n, qw[:, cols])
        queries[:, cols] = (q.astype(BF16).astype(F32) * scale).astype(BF16)
        for j in range(2):
            kk = k[:, j * LANES : (j + 1) * LANES]
            vv = v[:, j * LANES : (j + 1) * LANES]
            keys[4 * i + 2 * j] = jnp.where(low, kk, 0.0).astype(BF16)
            keys[4 * i + 2 * j + 1] = jnp.where(low, 0.0, kk).astype(BF16)
            values[4 * i + 2 * j] = jnp.where(low, vv, 1.0).astype(BF16)
            values[4 * i + 2 * j + 1] = jnp.where(low, 1.0, vv).astype(BF16)
        return carry

    lax.fori_loop(0, features // 256, project, 0)

    def attend(q2, head, count, offset):
        s = dot_t(q2, keys[head, :count, :]) + offset
        top = jnp.max(s, axis=1, keepdims=True)
        w = jnp.exp(s - top).astype(BF16)
        return dot(w, values[head, :count, :])

    def join(first, second):
        is_low = lax.broadcasted_iota(jnp.int32, first.shape, 1) < LANES // 2
        total = pltpu.roll(jnp.where(is_low, second, first), LANES // 2, 1)
        return (jnp.where(is_low, first, second) / total).astype(BF16)

    step_rows = 256

    def history_pair(p, carry):
        cols = pl.ds(pl.multiple_of(p * LANES, LANES), LANES)
        for r in range(0, events, step_rows):
            q2 = queries[r : r + step_rows, cols]
            count = r + step_rows
            offset = bias[r : r + step_rows, :count]
            context[r : r + step_rows, cols] = join(
                attend(q2, 2 * p, count, offset), attend(q2, 2 * p + 1, count, offset)
            )
        return carry

    lax.fori_loop(0, pairs, history_pair, 0)
    loads[3].wait()

    def history_out(i, carry):
        cols = pl.ds(pl.multiple_of(i * 256, 256), 256)
        new[:, cols] = (hist[:, cols].astype(F32) + dot(context[...], ow[:, cols])).astype(BF16)
        return carry

    lax.fori_loop(0, features // 256, history_out, 0)
    store = pltpu.make_async_copy(new, new_hbm.at[0], load_sem.at[4])
    store.start()

    chunks = slots // chunk
    per_chunk = chunk // cap

    def candidate_chunk(c, carry):
        which = lax.rem(half * (chunks // 2) + c, chunks)

        def arrive(i, inner):
            peer = which * per_chunk + i

            @pl.when(peer != me)
            def _():
                receiving(peer).wait_recv()

            return inner

        lax.fori_loop(0, per_chunk, arrive, 0)
        here = pl.ds(pl.multiple_of(which * chunk, chunk), chunk)
        n = normed_rows(inbox[here, :])
        q = dot(n, qw[...])
        cand_queries[...] = (q.astype(BF16).astype(F32) * scale).astype(BF16)

        def candidate_pair(p, inner):
            cols = pl.ds(pl.multiple_of(p * LANES, LANES), LANES)
            q2 = cand_queries[:, cols]
            offset = bias[events - 1 : events, :]
            cand_context[:, cols] = join(
                attend(q2, 2 * p, events, offset), attend(q2, 2 * p + 1, events, offset)
            )
            return inner

        lax.fori_loop(0, pairs, candidate_pair, 0)
        combined = inbox[here, :].astype(F32) + dot(cand_context[...], ow[...])
        logits = dot_t(head_ref[...], normed_rows(combined))
        for t in range(chunk // LANES):
            logit_out[which * (chunk // LANES) + t] = logits[:8, t * LANES : (t + 1) * LANES]
        return carry

    lax.fori_loop(0, chunks, candidate_chunk, 0)

    per_tile = LANES // cap

    def returning(peer):
        return pltpu.make_async_remote_copy(
            src_ref=logit_out.at[peer // per_tile],
            dst_ref=logit_in.at[me],
            send_sem=back_send_sem.at[peer],
            recv_sem=back_recv_sem.at[me],
            device_id={"users": peer},
            device_id_type=MESH,
        )

    def coming_back(peer):
        return pltpu.make_async_remote_copy(
            src_ref=logit_out.at[peer // per_tile],
            dst_ref=logit_in.at[peer],
            send_sem=back_send_sem.at[peer],
            recv_sem=back_recv_sem.at[peer],
            device_id={"users": peer},
            device_id_type=MESH,
        )

    def send_back(i, carry):
        returning(lax.rem(me + half_peers + i, peers)).start()
        return carry

    lax.fori_loop(0, half_peers, send_back, 0)

    def send_back_rest(i, carry):
        returning(lax.rem(me + i, peers)).start()
        return carry

    lax.fori_loop(1, half_peers, send_back_rest, 0)
    logit_in[me] = logit_out[me // per_tile]

    def back_arrive(i, carry):
        coming_back(lax.rem(me + i, peers)).wait_recv()
        return carry

    lax.fori_loop(1, peers, back_arrive, 0)

    lane = lax.broadcasted_iota(jnp.int32, (rows, LANES), 1).astype(F32)
    wanted = lane == rank_col + (lax.rem(me, per_tile) * cap).astype(F32)

    def pick(u, total):
        tile = logit_in[u]
        value = jnp.where(
            task_col == 0.0, tile[0:1], jnp.where(task_col == 1.0, tile[1:2], tile[2:3])
        )
        return jnp.where(user_col == u.astype(F32), value, total)

    picked = lax.fori_loop(0, peers, pick, jnp.zeros((rows, LANES), F32))
    score_col = jnp.sum(jnp.where(wanted, picked, 0.0), axis=1, keepdims=True)
    score_ref[...] = jnp.sum(jnp.where(eye, score_col, 0.0), axis=0, keepdims=True)

    def sent(i, carry):
        peer = lax.rem(me + i, peers)
        sending(peer).wait_send()
        returning(peer).wait_send()
        return carry

    lax.fori_loop(1, peers, sent, 0)
    store.wait()


def on_device(
    history,
    hist_len,
    candidates,
    cand_user,
    cand_task,
    kv_weight,
    query_weight,
    out_weight,
    head_weight,
):
    peers = lax.axis_size("users")
    rows, features = candidates.shape
    events = history.shape[1]
    cap = max(16, 2 * rows // peers)
    slots = peers * cap
    chunk = min(256, slots // 2)
    head_rows = jnp.pad(head_weight.T, ((0, 16 - head_weight.shape[1]), (0, 0)))
    vmem = pl.BlockSpec(memory_space=pltpu.VMEM)
    anywhere = pl.BlockSpec(memory_space=pl.ANY)
    new_history, scores = pl.pallas_call(
        functools.partial(kernel, peers, cap, chunk),
        out_shape=(
            jax.ShapeDtypeStruct(history.shape, history.dtype),
            jax.ShapeDtypeStruct((1, rows), F32),
        ),
        in_specs=[pl.BlockSpec(memory_space=pltpu.SMEM)] + [vmem] * 4 + [anywhere] * 4,
        out_specs=(anywhere, vmem),
        scratch_shapes=[
            pltpu.VMEM((events, features), BF16),
            pltpu.VMEM((features, 2 * features), BF16),
            pltpu.VMEM((features, features), BF16),
            pltpu.VMEM((features, features), BF16),
            pltpu.VMEM((events, features), BF16),
            pltpu.VMEM((events, features), BF16),
            pltpu.VMEM((HEADS, events, LANES), BF16),
            pltpu.VMEM((HEADS, events, LANES), BF16),
            pltpu.VMEM((events, features), BF16),
            pltpu.VMEM((events, features), BF16),
            pltpu.VMEM((events, events), F32),
            pltpu.VMEM((slots, features), BF16),
            pltpu.VMEM((slots, features), BF16),
            pltpu.VMEM((chunk, features), BF16),
            pltpu.VMEM((chunk, features), BF16),
            pltpu.VMEM((slots // LANES, 8, LANES), F32),
            pltpu.VMEM((peers, 8, LANES), F32),
            pltpu.SemaphoreType.DMA((5,)),
            pltpu.SemaphoreType.DMA((peers,)),
            pltpu.SemaphoreType.DMA((peers,)),
            pltpu.SemaphoreType.DMA((peers,)),
            pltpu.SemaphoreType.DMA((peers,)),
        ],
        compiler_params=pltpu.CompilerParams(
            collective_id=0, has_side_effects=True, vmem_limit_bytes=48 * 1024 * 1024
        ),
    )(
        hist_len,
        cand_user.reshape(1, rows),
        cand_task.reshape(1, rows),
        candidates,
        head_rows,
        history,
        kv_weight,
        query_weight,
        out_weight,
    )
    return new_history, scores.reshape(rows)


def solution(mesh):
    both = ("groups", "users")
    placed = (
        P(both, None, None),
        P(both),
        P(both, None),
        P(both, None),
        P(both),
        P(),
        P(),
        P(),
        P(),
    )
    return jax.shard_map(
        on_device,
        mesh=mesh,
        in_specs=placed,
        out_specs=(P(both, None, None), P(both)),
        check_vma=False,
    )
```

```python
import functools

import jax
import jax.numpy as jnp
from jax import lax
from jax.experimental import pallas as pl
from jax.experimental.pallas import tpu as pltpu
from jax.sharding import PartitionSpec as P

HEADS = 16
LANES = 128
EPSILON = 1e-06
NEG = -1e30
F32 = jnp.float32
BF16 = jnp.bfloat16
MESH = pl.DeviceIdType.MESH


def normed_rows(values):
    values = values.astype(F32)
    mean = jnp.mean(values * values, axis=-1, keepdims=True)
    return (values * lax.rsqrt(mean + EPSILON)).astype(BF16)


def dot_t(a, b):
    return lax.dot_general(a, b, (((1,), (1,)), ((), ())), preferred_element_type=F32)


def dot(a, b):
    return jnp.dot(a, b, preferred_element_type=F32)


def kernel(
    peers,
    cap,
    chunk,
    len_ref,
    user_hbm,
    task_hbm,
    cand_hbm,
    head_hbm,
    hist_hbm,
    kvw_hbm,
    qw_hbm,
    ow_hbm,
    new_hbm,
    score_ref,
    user_ref,
    task_ref,
    cand_ref,
    head_ref,
    hist,
    kvw,
    qw,
    ow,
    new,
    normed,
    keys,
    values,
    queries,
    context,
    bias,
    outbox,
    inbox,
    cand_queries,
    cand_context,
    logit_out,
    logit_in,
    load_sem,
    send_sem,
    recv_sem,
    back_send_sem,
    back_recv_sem,
):
    me = lax.axis_index("users")
    half_peers = peers // 2
    events, features = hist.shape
    slots = inbox.shape[0]
    rows = cand_ref.shape[0]
    pairs = features // LANES
    tasks = head_ref.shape[0]

    loads = [
        pltpu.make_async_copy(src, dst, load_sem.at[i])
        for i, (src, dst) in enumerate(
            (
                (user_hbm, user_ref),
                (task_hbm, task_ref),
                (cand_hbm, cand_ref),
                (hist_hbm.at[0], hist),
                (kvw_hbm, kvw),
                (qw_hbm, qw),
                (ow_hbm, ow),
                (head_hbm, head_ref),
            )
        )
    ]
    for load in loads:
        load.start()

    barrier = pltpu.get_barrier_semaphore()

    def greet(i, carry):
        pl.semaphore_signal(
            barrier, inc=1, device_id={"users": lax.rem(me + i, peers)}, device_id_type=MESH
        )
        return carry

    lax.fori_loop(1, peers, greet, 0)

    loads[0].wait()
    loads[1].wait()
    row_id = lax.broadcasted_iota(jnp.int32, (rows, rows), 0)
    col_id = lax.broadcasted_iota(jnp.int32, (rows, rows), 1)
    eye = row_id == col_id
    user_row = user_ref[...].astype(F32)
    task_row = task_ref[...].astype(F32)
    user_col = jnp.sum(jnp.where(eye, user_row, 0.0), axis=1, keepdims=True)
    task_col = jnp.sum(jnp.where(eye, task_row, 0.0), axis=1, keepdims=True)
    same = user_col == user_row
    rank_row = jnp.sum(jnp.where(same & (row_id < col_id), 1.0, 0.0), axis=0, keepdims=True)
    rank_col = jnp.sum(jnp.where(same & (col_id < row_id), 1.0, 0.0), axis=1, keepdims=True)
    target_row = user_row * cap + rank_row

    def pack(first):
        slot = (lax.broadcasted_iota(jnp.int32, (chunk, rows), 0) + first).astype(F32)
        chosen = jnp.where(slot == target_row, 1.0, 0.0).astype(BF16)
        outbox[pl.ds(first, chunk), :] = dot(chosen, cand_ref[...]).astype(BF16)

    def block(ref, peer):
        return ref.at[pl.ds(pl.multiple_of(peer * cap, cap), cap), :]

    def sending(peer):
        return pltpu.make_async_remote_copy(
            src_ref=block(outbox, peer),
            dst_ref=block(inbox, me),
            send_sem=send_sem.at[peer],
            recv_sem=recv_sem.at[me],
            device_id={"users": peer},
            device_id_type=MESH,
        )

    def receiving(peer):
        return pltpu.make_async_remote_copy(
            src_ref=block(outbox, peer),
            dst_ref=block(inbox, peer),
            send_sem=send_sem.at[peer],
            recv_sem=recv_sem.at[peer],
            device_id={"users": peer},
            device_id_type=MESH,
        )

    groups = slots // chunk
    members = peers // groups
    part = groups // 2
    group = me // members
    group_half, group_rest = group // part, lax.rem(group, part)

    def partner(phase, sign):
        side = lax.rem(group_half + phase // part, 2)
        return side * part + lax.rem(group_rest + part + sign * lax.rem(phase, part), part)

    loads[2].wait()

    def pack_phase(phase):
        pack(pl.multiple_of(partner(phase, 1) * chunk, chunk))

    def send_phase(phase):
        first = partner(phase, 1) * members

        def send_one(i, carry):
            peer = first + lax.rem(me + i, members)

            @pl.when(peer != me)
            def _():
                sending(peer).start()

            return carry

        lax.fori_loop(0, members, send_one, 0)

    def order(i):
        return lax.rem(i + part, groups)

    pack_phase(order(0))
    pl.semaphore_wait(barrier, peers - 1)
    send_phase(order(0))

    def pack_and_send(i, carry):
        pack_phase(order(i))
        send_phase(order(i))
        return carry

    lax.fori_loop(1, groups, pack_and_send, 0)
    own = pl.ds(pl.multiple_of(me * cap, cap), cap)
    inbox[own, :] = outbox[own, :]

    loads[3].wait()
    normed[...] = normed_rows(hist[...])
    event_row = lax.broadcasted_iota(jnp.int32, (events, events), 0)
    event_col = lax.broadcasted_iota(jnp.int32, (events, events), 1)
    allowed = (event_col <= event_row) & (event_col < len_ref[0])
    bias[...] = jnp.where(allowed, 0.0, NEG)
    scale = 0.125
    low = lax.broadcasted_iota(jnp.int32, (events, LANES), 1) < LANES // 2
    loads[4].wait()
    loads[5].wait()

    def project(i, carry):
        cols = pl.ds(pl.multiple_of(i * 256, 256), 256)
        later = pl.ds(pl.multiple_of(features + i * 256, 256), 256)
        n = normed[...]
        k = dot(n, kvw[:, cols])
        v = dot(n, kvw[:, later])
        q = dot(n, qw[:, cols])
        queries[:, cols] = (q.astype(BF16).astype(F32) * scale).astype(BF16)
        for j in range(2):
            kk = k[:, j * LANES : (j + 1) * LANES]
            vv = v[:, j * LANES : (j + 1) * LANES]
            keys[4 * i + 2 * j] = jnp.where(low, kk, 0.0).astype(BF16)
            keys[4 * i + 2 * j + 1] = jnp.where(low, 0.0, kk).astype(BF16)
            values[4 * i + 2 * j] = jnp.where(low, vv, 0.0).astype(BF16)
            values[4 * i + 2 * j + 1] = jnp.where(low, 0.0, vv).astype(BF16)
        return carry

    lax.fori_loop(0, features // 256, project, 0)

    def attend(q2, head, count, offset):
        s = dot_t(q2, keys[head, :count, :]) + offset
        top = jnp.max(s, axis=1, keepdims=True)
        raised = jnp.exp(s - top)
        share = 1.0 / jnp.sum(raised, axis=1, keepdims=True)
        return dot((raised * share).astype(BF16), values[head, :count, :])

    def attend_pair(q2, p, count, offset):
        both = attend(q2, 2 * p, count, offset) + attend(q2, 2 * p + 1, count, offset)
        return both.astype(BF16)

    step_rows = 256

    def history_pair(p, carry):
        cols = pl.ds(pl.multiple_of(p * LANES, LANES), LANES)
        for r in range(0, events, step_rows):
            q2 = queries[r : r + step_rows, cols]
            count = r + step_rows
            offset = bias[r : r + step_rows, :count]
            context[r : r + step_rows, cols] = attend_pair(q2, p, count, offset)
        return carry

    lax.fori_loop(0, pairs, history_pair, 0, unroll=4)
    loads[6].wait()

    def history_out(i, carry):
        cols = pl.ds(pl.multiple_of(i * 256, 256), 256)
        new[:, cols] = (hist[:, cols].astype(F32) + dot(context[...], ow[:, cols])).astype(BF16)
        return carry

    lax.fori_loop(0, features // 256, history_out, 0)
    store = pltpu.make_async_copy(new, new_hbm.at[0], load_sem.at[8])
    store.start()

    loads[7].wait()

    def candidate_chunk(c, carry):
        which = partner(c, -1)

        def arrive(i, inner):
            peer = which * members + i

            @pl.when(peer != me)
            def _():
                receiving(peer).wait_recv()

            return inner

        lax.fori_loop(0, members, arrive, 0)
        here = pl.ds(pl.multiple_of(which * chunk, chunk), chunk)
        n = normed_rows(inbox[here, :])
        q = dot(n, qw[...])
        cand_queries[...] = (q.astype(BF16).astype(F32) * scale).astype(BF16)

        def candidate_pair(p, inner):
            cols = pl.ds(pl.multiple_of(p * LANES, LANES), LANES)
            q2 = cand_queries[:, cols]
            offset = bias[events - 1 : events, :]
            cand_context[:, cols] = attend_pair(q2, p, events, offset)
            return inner

        lax.fori_loop(0, pairs, candidate_pair, 0, unroll=4)
        combined = inbox[here, :].astype(F32) + dot(cand_context[...], ow[...])
        logits = dot_t(head_ref[...], normed_rows(combined))
        for t in range(chunk // LANES):
            logit_out[which * (chunk // LANES) + t, :tasks, :] = logits[
                :, t * LANES : (t + 1) * LANES
            ]
        return carry

    lax.fori_loop(0, groups, candidate_chunk, 0)

    per_tile = LANES // cap

    def returning(peer):
        return pltpu.make_async_remote_copy(
            src_ref=logit_out.at[peer // per_tile],
            dst_ref=logit_in.at[me],
            send_sem=back_send_sem.at[peer],
            recv_sem=back_recv_sem.at[me],
            device_id={"users": peer},
            device_id_type=MESH,
        )

    def coming_back(peer):
        return pltpu.make_async_remote_copy(
            src_ref=logit_out.at[peer // per_tile],
            dst_ref=logit_in.at[peer],
            send_sem=back_send_sem.at[peer],
            recv_sem=back_recv_sem.at[peer],
            device_id={"users": peer},
            device_id_type=MESH,
        )

    def send_back(i, carry):
        returning(lax.rem(me + half_peers + i, peers)).start()
        return carry

    lax.fori_loop(0, half_peers, send_back, 0)

    def send_back_rest(i, carry):
        returning(lax.rem(me + i, peers)).start()
        return carry

    lax.fori_loop(1, half_peers, send_back_rest, 0)
    logit_in[me] = logit_out[me // per_tile]

    def back_arrive(i, carry):
        coming_back(lax.rem(me + i, peers)).wait_recv()
        return carry

    lax.fori_loop(1, peers, back_arrive, 0)

    lane = lax.broadcasted_iota(jnp.int32, (rows, LANES), 1).astype(F32)
    wanted = lane == rank_col + (lax.rem(me, per_tile) * cap).astype(F32)

    def pick(u, total):
        tile = logit_in[u]
        value = jnp.where(
            task_col == 0.0, tile[0:1], jnp.where(task_col == 1.0, tile[1:2], tile[2:3])
        )
        return jnp.where(user_col == u.astype(F32), value, total)

    picked = lax.fori_loop(0, peers, pick, jnp.zeros((rows, LANES), F32))
    score_col = jnp.sum(jnp.where(wanted, picked, 0.0), axis=1, keepdims=True)
    score_ref[...] = jnp.sum(jnp.where(eye, score_col, 0.0), axis=0, keepdims=True)

    def sent(i, carry):
        peer = lax.rem(me + i, peers)
        sending(peer).wait_send()
        returning(peer).wait_send()
        return carry

    lax.fori_loop(1, peers, sent, 0)
    store.wait()


def on_device(
    history,
    hist_len,
    candidates,
    cand_user,
    cand_task,
    kv_weight,
    query_weight,
    out_weight,
    head_weight,
):
    peers = lax.axis_size("users")
    rows, features = candidates.shape
    events = history.shape[1]
    cap = max(16, 2 * rows // peers)
    slots = peers * cap
    chunk = 256
    vmem = pl.BlockSpec(memory_space=pltpu.VMEM)
    anywhere = pl.BlockSpec(memory_space=pl.ANY)
    new_history, scores = pl.pallas_call(
        functools.partial(kernel, peers, cap, chunk),
        out_shape=(
            jax.ShapeDtypeStruct(history.shape, history.dtype),
            jax.ShapeDtypeStruct((1, rows), F32),
        ),
        in_specs=[pl.BlockSpec(memory_space=pltpu.SMEM)] + [anywhere] * 8,
        out_specs=(anywhere, vmem),
        scratch_shapes=[
            pltpu.VMEM((1, rows), jnp.int32),
            pltpu.VMEM((1, rows), jnp.int32),
            pltpu.VMEM((rows, features), BF16),
            pltpu.VMEM((head_weight.shape[1], features), BF16),
            pltpu.VMEM((events, features), BF16),
            pltpu.VMEM((features, 2 * features), BF16),
            pltpu.VMEM((features, features), BF16),
            pltpu.VMEM((features, features), BF16),
            pltpu.VMEM((events, features), BF16),
            pltpu.VMEM((events, features), BF16),
            pltpu.VMEM((HEADS, events, LANES), BF16),
            pltpu.VMEM((HEADS, events, LANES), BF16),
            pltpu.VMEM((events, features), BF16),
            pltpu.VMEM((events, features), BF16),
            pltpu.VMEM((events, events), F32),
            pltpu.VMEM((slots, features), BF16),
            pltpu.VMEM((slots, features), BF16),
            pltpu.VMEM((chunk, features), BF16),
            pltpu.VMEM((chunk, features), BF16),
            pltpu.VMEM((slots // LANES, 8, LANES), F32),
            pltpu.VMEM((peers, 8, LANES), F32),
            pltpu.SemaphoreType.DMA((9,)),
            pltpu.SemaphoreType.DMA((peers,)),
            pltpu.SemaphoreType.DMA((peers,)),
            pltpu.SemaphoreType.DMA((peers,)),
            pltpu.SemaphoreType.DMA((peers,)),
        ],
        compiler_params=pltpu.CompilerParams(
            collective_id=0, has_side_effects=True, vmem_limit_bytes=60 * 1024 * 1024
        ),
    )(
        hist_len,
        cand_user.reshape(1, rows),
        cand_task.reshape(1, rows),
        candidates,
        head_weight.T,
        history,
        kv_weight,
        query_weight,
        out_weight,
    )
    return new_history, scores.reshape(rows)


def solution(mesh):
    both = ("groups", "users")
    placed = (
        P(both, None, None),
        P(both),
        P(both, None),
        P(both, None),
        P(both),
        P(),
        P(),
        P(),
        P(),
    )
    return jax.shard_map(
        on_device,
        mesh=mesh,
        in_specs=placed,
        out_specs=(P(both, None, None), P(both)),
        check_vma=False,
    )
```

```python
import functools

import jax
import jax.numpy as jnp
from jax import lax
from jax.experimental import pallas as pl
from jax.experimental.pallas import tpu as pltpu
from jax.sharding import PartitionSpec as P

HEADS = 16
LANES = 128
EPSILON = 1e-06
NEG = -1e30
F32 = jnp.float32
BF16 = jnp.bfloat16
MESH = pl.DeviceIdType.MESH


def normed_rows(values):
    values = values.astype(F32)
    mean = jnp.mean(values * values, axis=-1, keepdims=True)
    return (values * lax.rsqrt(mean + EPSILON)).astype(BF16)


def dot_t(a, b):
    return lax.dot_general(a, b, (((1,), (1,)), ((), ())), preferred_element_type=F32)


def dot(a, b):
    return jnp.dot(a, b, preferred_element_type=F32)


def kernel(
    peers,
    cap,
    chunk,
    len_ref,
    user_hbm,
    task_hbm,
    cand_hbm,
    head_hbm,
    hist_hbm,
    kvw_hbm,
    qw_hbm,
    ow_hbm,
    new_hbm,
    score_ref,
    user_ref,
    task_ref,
    cand_ref,
    head_ref,
    hist,
    kvw,
    qw,
    ow,
    new,
    normed,
    keys,
    values,
    queries,
    context,
    bias,
    outbox,
    inbox,
    cand_queries,
    cand_context,
    logit_out,
    logit_in,
    load_sem,
    send_sem,
    recv_sem,
    back_send_sem,
    back_recv_sem,
):
    me = lax.axis_index("users")
    half_peers = peers // 2
    events, features = hist.shape
    slots = inbox.shape[0]
    rows = cand_ref.shape[0]
    pairs = features // LANES
    tasks = head_ref.shape[0]

    loads = [
        pltpu.make_async_copy(src, dst, load_sem.at[i])
        for i, (src, dst) in enumerate(
            (
                (user_hbm, user_ref),
                (task_hbm, task_ref),
                (cand_hbm, cand_ref),
                (hist_hbm.at[0], hist),
                (kvw_hbm, kvw),
                (qw_hbm, qw),
                (ow_hbm, ow),
                (head_hbm, head_ref),
            )
        )
    ]
    for load in loads:
        load.start()

    barrier = pltpu.get_barrier_semaphore()

    def greet(i, carry):
        pl.semaphore_signal(
            barrier, inc=1, device_id={"users": lax.rem(me + i, peers)}, device_id_type=MESH
        )
        return carry

    lax.fori_loop(1, peers, greet, 0)

    loads[0].wait()
    loads[1].wait()
    row_id = lax.broadcasted_iota(jnp.int32, (rows, rows), 0)
    col_id = lax.broadcasted_iota(jnp.int32, (rows, rows), 1)
    eye = row_id == col_id
    user_row = user_ref[...].astype(F32)
    task_row = task_ref[...].astype(F32)
    user_col = jnp.sum(jnp.where(eye, user_row, 0.0), axis=1, keepdims=True)
    task_col = jnp.sum(jnp.where(eye, task_row, 0.0), axis=1, keepdims=True)
    same = user_col == user_row
    rank_row = jnp.sum(jnp.where(same & (row_id < col_id), 1.0, 0.0), axis=0, keepdims=True)
    rank_col = jnp.sum(jnp.where(same & (col_id < row_id), 1.0, 0.0), axis=1, keepdims=True)
    target_row = user_row * cap + rank_row

    def pack(first):
        slot = (lax.broadcasted_iota(jnp.int32, (chunk, rows), 0) + first).astype(F32)
        chosen = jnp.where(slot == target_row, 1.0, 0.0).astype(BF16)
        outbox[pl.ds(first, chunk), :] = dot(chosen, cand_ref[...]).astype(BF16)

    def block(ref, peer):
        return ref.at[pl.ds(pl.multiple_of(peer * cap, cap), cap), :]

    def sending(peer):
        return pltpu.make_async_remote_copy(
            src_ref=block(outbox, peer),
            dst_ref=block(inbox, me),
            send_sem=send_sem.at[peer],
            recv_sem=recv_sem.at[me],
            device_id={"users": peer},
            device_id_type=MESH,
        )

    def receiving(peer):
        return pltpu.make_async_remote_copy(
            src_ref=block(outbox, peer),
            dst_ref=block(inbox, peer),
            send_sem=send_sem.at[peer],
            recv_sem=recv_sem.at[peer],
            device_id={"users": peer},
            device_id_type=MESH,
        )

    groups = slots // chunk
    members = peers // groups
    part = groups // 2
    group = me // members
    group_half, group_rest = group // part, lax.rem(group, part)

    def partner(phase, sign):
        side = lax.rem(group_half + phase // part, 2)
        return side * part + lax.rem(group_rest + part + sign * lax.rem(phase, part), part)

    loads[2].wait()

    def pack_phase(phase):
        pack(pl.multiple_of(partner(phase, 1) * chunk, chunk))

    def send_phase(phase):
        first = partner(phase, 1) * members

        def send_one(i, carry):
            peer = first + lax.rem(me + i, members)

            @pl.when(peer != me)
            def _():
                sending(peer).start()

            return carry

        lax.fori_loop(0, members, send_one, 0)

    def order(i):
        return i

    pack_phase(order(0))
    pl.semaphore_wait(barrier, peers - 1)
    send_phase(order(0))

    def pack_and_send(i, carry):
        pack_phase(order(i))
        send_phase(order(i))
        return carry

    lax.fori_loop(1, groups, pack_and_send, 0)
    own = pl.ds(pl.multiple_of(me * cap, cap), cap)
    inbox[own, :] = outbox[own, :]

    loads[3].wait()
    normed[...] = normed_rows(hist[...])
    event_row = lax.broadcasted_iota(jnp.int32, (events, events), 0)
    event_col = lax.broadcasted_iota(jnp.int32, (events, events), 1)
    allowed = (event_col <= event_row) & (event_col < len_ref[0])
    bias[...] = jnp.where(allowed, 0.0, NEG)
    scale = 0.125
    low = lax.broadcasted_iota(jnp.int32, (events, LANES), 1) < LANES // 2
    loads[4].wait()
    loads[5].wait()

    def project(i, carry):
        cols = pl.ds(pl.multiple_of(i * 256, 256), 256)
        later = pl.ds(pl.multiple_of(features + i * 256, 256), 256)
        n = normed[...]
        k = dot(n, kvw[:, cols])
        v = dot(n, kvw[:, later])
        q = dot(n, qw[:, cols])
        queries[:, cols] = (q.astype(BF16).astype(F32) * scale).astype(BF16)
        for j in range(2):
            kk = k[:, j * LANES : (j + 1) * LANES]
            vv = v[:, j * LANES : (j + 1) * LANES]
            keys[4 * i + 2 * j] = jnp.where(low, kk, 0.0).astype(BF16)
            keys[4 * i + 2 * j + 1] = jnp.where(low, 0.0, kk).astype(BF16)
            values[4 * i + 2 * j] = jnp.where(low, vv, 0.0).astype(BF16)
            values[4 * i + 2 * j + 1] = jnp.where(low, 0.0, vv).astype(BF16)
        return carry

    lax.fori_loop(0, features // 256, project, 0)

    def attend(q2, head, count, offset):
        s = dot_t(q2, keys[head, :count, :]) + offset
        top = jnp.max(s, axis=1, keepdims=True)
        raised = jnp.exp(s - top)
        share = 1.0 / jnp.sum(raised, axis=1, keepdims=True)
        return dot((raised * share).astype(BF16), values[head, :count, :])

    def attend_pair(q2, p, count, offset):
        parts = []
        for head in (2 * p, 2 * p + 1):
            s = dot_t(q2, keys[head, :count, :]) + offset
            raised = jnp.exp(s - jnp.max(s, axis=1, keepdims=True))
            share = 1.0 / jnp.sum(raised, axis=1, keepdims=True)
            parts.append((raised * share).astype(BF16))
        pair_values = jnp.concatenate(
            [values[2 * p, :count, :], values[2 * p + 1, :count, :]], axis=0
        )
        return dot(jnp.concatenate(parts, axis=1), pair_values).astype(BF16)

    step_rows = 256

    def history_pair(p, carry):
        cols = pl.ds(pl.multiple_of(p * LANES, LANES), LANES)
        for r in range(0, events, step_rows):
            q2 = queries[r : r + step_rows, cols]
            count = r + step_rows
            offset = bias[r : r + step_rows, :count]
            context[r : r + step_rows, cols] = attend_pair(q2, p, count, offset)
        return carry

    lax.fori_loop(0, pairs, history_pair, 0, unroll=8)
    loads[6].wait()

    def history_out(i, carry):
        cols = pl.ds(pl.multiple_of(i * 256, 256), 256)
        new[:, cols] = (hist[:, cols].astype(F32) + dot(context[...], ow[:, cols])).astype(BF16)
        return carry

    lax.fori_loop(0, features // 256, history_out, 0)
    store = pltpu.make_async_copy(new, new_hbm.at[0], load_sem.at[8])
    store.start()

    loads[7].wait()

    def candidate_chunk(c, carry):
        which = partner(c, -1)

        def arrive(i, inner):
            peer = which * members + i

            @pl.when(peer != me)
            def _():
                receiving(peer).wait_recv()

            return inner

        lax.fori_loop(0, members, arrive, 0)
        here = pl.ds(pl.multiple_of(which * chunk, chunk), chunk)
        n = normed_rows(inbox[here, :])
        q = dot(n, qw[...])
        cand_queries[...] = (q.astype(BF16).astype(F32) * scale).astype(BF16)

        def candidate_pair(p, inner):
            cols = pl.ds(pl.multiple_of(p * LANES, LANES), LANES)
            q2 = cand_queries[:, cols]
            offset = bias[events - 1 : events, :]
            cand_context[:, cols] = attend_pair(q2, p, events, offset)
            return inner

        lax.fori_loop(0, pairs, candidate_pair, 0, unroll=8)
        combined = inbox[here, :].astype(F32) + dot(cand_context[...], ow[...])
        logits = dot_t(head_ref[...], normed_rows(combined))
        for t in range(chunk // LANES):
            logit_out[which * (chunk // LANES) + t, :tasks, :] = logits[
                :, t * LANES : (t + 1) * LANES
            ]
        return carry

    lax.fori_loop(0, groups, candidate_chunk, 0)

    per_tile = LANES // cap

    def returning(peer):
        return pltpu.make_async_remote_copy(
            src_ref=logit_out.at[peer // per_tile],
            dst_ref=logit_in.at[me],
            send_sem=back_send_sem.at[peer],
            recv_sem=back_recv_sem.at[me],
            device_id={"users": peer},
            device_id_type=MESH,
        )

    def coming_back(peer):
        return pltpu.make_async_remote_copy(
            src_ref=logit_out.at[peer // per_tile],
            dst_ref=logit_in.at[peer],
            send_sem=back_send_sem.at[peer],
            recv_sem=back_recv_sem.at[peer],
            device_id={"users": peer},
            device_id_type=MESH,
        )

    def send_back(i, carry):
        returning(lax.rem(me + half_peers + i, peers)).start()
        return carry

    lax.fori_loop(0, half_peers, send_back, 0)

    def send_back_rest(i, carry):
        returning(lax.rem(me + i, peers)).start()
        return carry

    lax.fori_loop(1, half_peers, send_back_rest, 0)
    logit_in[me] = logit_out[me // per_tile]

    def back_arrive(i, carry):
        coming_back(lax.rem(me + i, peers)).wait_recv()
        return carry

    lax.fori_loop(1, peers, back_arrive, 0)

    lane = lax.broadcasted_iota(jnp.int32, (rows, LANES), 1).astype(F32)
    wanted = lane == rank_col + (lax.rem(me, per_tile) * cap).astype(F32)

    def pick(u, total):
        tile = logit_in[u]
        value = jnp.where(
            task_col == 0.0, tile[0:1], jnp.where(task_col == 1.0, tile[1:2], tile[2:3])
        )
        return jnp.where(user_col == u.astype(F32), value, total)

    picked = lax.fori_loop(0, peers, pick, jnp.zeros((rows, LANES), F32))
    score_col = jnp.sum(jnp.where(wanted, picked, 0.0), axis=1, keepdims=True)
    score_ref[...] = jnp.sum(jnp.where(eye, score_col, 0.0), axis=0, keepdims=True)

    def sent(i, carry):
        peer = lax.rem(me + i, peers)
        sending(peer).wait_send()
        returning(peer).wait_send()
        return carry

    lax.fori_loop(1, peers, sent, 0)
    store.wait()


def on_device(
    history,
    hist_len,
    candidates,
    cand_user,
    cand_task,
    kv_weight,
    query_weight,
    out_weight,
    head_weight,
):
    peers = lax.axis_size("users")
    rows, features = candidates.shape
    events = history.shape[1]
    cap = max(16, 2 * rows // peers)
    slots = peers * cap
    chunk = 256
    vmem = pl.BlockSpec(memory_space=pltpu.VMEM)
    anywhere = pl.BlockSpec(memory_space=pl.ANY)
    new_history, scores = pl.pallas_call(
        functools.partial(kernel, peers, cap, chunk),
        out_shape=(
            jax.ShapeDtypeStruct(history.shape, history.dtype),
            jax.ShapeDtypeStruct((1, rows), F32),
        ),
        in_specs=[pl.BlockSpec(memory_space=pltpu.SMEM)] + [anywhere] * 8,
        out_specs=(anywhere, vmem),
        scratch_shapes=[
            pltpu.VMEM((1, rows), jnp.int32),
            pltpu.VMEM((1, rows), jnp.int32),
            pltpu.VMEM((rows, features), BF16),
            pltpu.VMEM((head_weight.shape[1], features), BF16),
            pltpu.VMEM((events, features), BF16),
            pltpu.VMEM((features, 2 * features), BF16),
            pltpu.VMEM((features, features), BF16),
            pltpu.VMEM((features, features), BF16),
            pltpu.VMEM((events, features), BF16),
            pltpu.VMEM((events, features), BF16),
            pltpu.VMEM((HEADS, events, LANES), BF16),
            pltpu.VMEM((HEADS, events, LANES), BF16),
            pltpu.VMEM((events, features), BF16),
            pltpu.VMEM((events, features), BF16),
            pltpu.VMEM((events, events), F32),
            pltpu.VMEM((slots, features), BF16),
            pltpu.VMEM((slots, features), BF16),
            pltpu.VMEM((chunk, features), BF16),
            pltpu.VMEM((chunk, features), BF16),
            pltpu.VMEM((slots // LANES, 8, LANES), F32),
            pltpu.VMEM((peers, 8, LANES), F32),
            pltpu.SemaphoreType.DMA((9,)),
            pltpu.SemaphoreType.DMA((peers,)),
            pltpu.SemaphoreType.DMA((peers,)),
            pltpu.SemaphoreType.DMA((peers,)),
            pltpu.SemaphoreType.DMA((peers,)),
        ],
        compiler_params=pltpu.CompilerParams(
            collective_id=0, has_side_effects=True, vmem_limit_bytes=60 * 1024 * 1024
        ),
    )(
        hist_len,
        cand_user.reshape(1, rows),
        cand_task.reshape(1, rows),
        candidates,
        head_weight.T,
        history,
        kv_weight,
        query_weight,
        out_weight,
    )
    return new_history, scores.reshape(rows)


def solution(mesh):
    both = ("groups", "users")
    placed = (
        P(both, None, None),
        P(both),
        P(both, None),
        P(both, None),
        P(both),
        P(),
        P(),
        P(),
        P(),
    )
    return jax.shard_map(
        on_device,
        mesh=mesh,
        in_specs=placed,
        out_specs=(P(both, None, None), P(both)),
        check_vma=False,
    )
```
